768 devices in a mesh: space: 24 (over z, x_lo), dp: 32 (over x_hi, y, core).
Axes of the slice: x: 4 (x_hi: 2, x_lo: 2; x = x_hi * 2 + x_lo), y: 8, z: 12, core: 2. Of those that a mesh axis runs over, the one named last changes fastest.
Arguments:
- windows_in: bfloat16 [32, 192, 64, 768], P('dp', 'space'), may hold values from -6 to 6
- cotangent: bfloat16 [32, 192, 64, 768], P('dp', 'space'), may hold values from -0.1796875 to 0.1796875
- wet_mask: int32 [32, 192, 64], P('dp', 'space'), may hold values from 0 to 1, as said below
- wet_count: int32 [32, 24], P('dp', 'space'), may hold values from 1 to 8, as said below
- qkv_weight: bfloat16 [768, 1152], replicated, may hold values from -0.21875 to 0.21875
- proj_weight: bfloat16 [768, 384], replicated, may hold values from -0.3125 to 0.3125
- score_bias: float32 [6, 64, 64], replicated, may hold values from -4 to 256
Outputs:
- windows_out: bfloat16 [32, 192, 64, 768], P('dp', 'space')
- input_grad: bfloat16 [32, 192, 64, 768], P('dp', 'space')
- proj_grad: float32 [294912], P(('space', 'dp'))
The draws below stay inside these ranges and needn't reach their ends.
Inputs may be any that keep to these rules, and one draw needn't show every extreme that they name: `wet_mask`: 1 marks a wet cell; every window slot has one or more wet cells. The wet windows of a tile fill its first slots; the later slots are land. Tiles t and t + 12 of a sample are matched partners: wet_count[b, t] + wet_count[b, t + 12] = 9.
All inputs are finite; a program needn't handle non-finite values.
Results may differ from the reference program's by a relative error of at most 0.0078.
Values may be sent and summed in bfloat16 or wider, within the bound.
No kernel may reach another device: no remote copies, remote signals or barrier semaphores. Data moves between devices by JAX's collectives and lax.ppermute only.
A program may use at most 32 MiB of HBM per device.

```python
import jax
import jax.numpy as jnp
from jax import lax

C = 768
HEADS = 6
CELLS = 64
WIN_DEV = 8
HD = 384
TILES = 24
WINDOWS = 192
BATCH = 32


def draw_wet_mask(key, part):
    key = jax.random.fold_in(key, 3)
    level_key, cell_key, pin_key = jax.random.split(key, 3)
    levels = jax.random.randint(level_key, (BATCH, WINDOWS, 1), 20, 101)
    rolled = jax.random.randint(cell_key, (BATCH, WINDOWS, CELLS), 0, 100)
    pinned = jax.random.randint(pin_key, (BATCH, WINDOWS, 1), 0, CELLS)
    cell_ids = jnp.arange(CELLS, dtype=jnp.int32)[None, None, :]
    return ((rolled < levels) | (cell_ids == pinned)).astype(jnp.int32)


def draw_wet_count(key, part):
    key = jax.random.fold_in(key, 5)
    order_key, flip_key = jax.random.split(key, 2)
    half_tiles = TILES // 2
    pair_total = BATCH * half_tiles
    ordering = jax.random.permutation(order_key, pair_total).astype(jnp.int32)
    first = (1 + ordering * WIN_DEV // pair_total).reshape(BATCH, half_tiles).astype(jnp.int32)
    second = (WIN_DEV + 1 - first).astype(jnp.int32)
    flipped = jax.random.randint(flip_key, (BATCH, half_tiles), 0, 2) > 0
    lower = jnp.where(flipped, second, first)
    upper = jnp.where(flipped, first, second)
    return jnp.concatenate([lower, upper], 1).astype(jnp.int32)


def draw_score_bias(key, part):
    key = jax.random.fold_in(key, 7)
    base_key = jax.random.fold_in(key, 0)
    return jnp.clip(jax.random.normal(base_key, (HEADS, CELLS, CELLS), jnp.float32), -4.0, 4.0)


def with_spikes(drawn, rng, source, target, parts, factor):
    def block_of(axis_at):
        return (jnp.arange(drawn.shape[axis_at]) // (drawn.shape[axis_at] // parts)).reshape((-1,) + (1,) * (drawn.ndim - 1 - axis_at))

    one_side = jax.random.permutation(rng, parts)[block_of(target)]
    other_side = (block_of(target) + parts // 2) % parts
    return jnp.where((block_of(source) == one_side) | (block_of(source) == other_side), factor * drawn, drawn)


def level_of(rng, extent, cuts, smallest, high):
    loudness, own = 1.0, jax.random.fold_in(rng, 6)
    for dim, blocks in cuts:
        draws = jnp.exp(jax.random.uniform(jax.random.fold_in(own, dim), (blocks,), jnp.float32, smallest / len(cuts), high / len(cuts)))
        loudness = loudness * jnp.repeat(draws, extent[dim] // blocks).reshape([-1 if axis == dim else 1 for axis in range(len(extent))])
    return loudness


def noise(own_key, extent, scale, most, cuts=(), held_as=jnp.bfloat16):
    drawn = jax.random.normal(own_key, extent, jnp.float32) * scale
    if len(cuts) > 0:
        drawn = level_of(own_key, extent, cuts, -0.22, 0.18) * drawn
    return jnp.clip(drawn, min=-most, max=most).astype(held_as)


def noise_with(stream_key, extent, deviation, most, shards, heavy, held_as=jnp.bfloat16):
    values = deviation * jax.random.normal(stream_key, extent, jnp.float32)
    if shards:
        values = values * level_of(stream_key, extent, shards, -0.22, 0.18)
    return jnp.clip(with_spikes(values, jax.random.fold_in(stream_key, 3), *heavy), -most, most).astype(held_as)


def setup_inputs(seed: int = 0) -> dict:
    splits = jax.random.split(jax.random.key(seed), 8)
    windows_in = noise(splits[0], (BATCH, WINDOWS, CELLS, C), 1.0, 6.0, ((0, 32), (1, 24)))
    cotangent = noise_with(splits[1], (BATCH, WINDOWS, CELLS, C), 0.03, 0.1796875, ((0, 32), (1, 24)), (1, 3, 24, 2.25))
    wet_mask = draw_wet_mask(jax.random.fold_in(splits[7], 71), 0)
    wet_count = draw_wet_count(jax.random.fold_in(splits[7], 71), 0)
    qkv_weight = noise(splits[4], (C, 3 * HD), C ** -0.5, 0.21875)
    proj_weight = noise(splits[5], (C, HD), HD ** -0.5, 0.3125)
    score_bias = draw_score_bias(jax.random.fold_in(splits[7], 71), 0)
    return {"windows_in": windows_in, "cotangent": cotangent, "wet_mask": wet_mask, "wet_count": wet_count, "qkv_weight": qkv_weight, "proj_weight": proj_weight, "score_bias": score_bias}


epsilon = 1e-05

def window_pass(tile_x, tile_g, wet_cells, live_rows, qkv_weight, proj_weight, score_bias):
    head_count = score_bias.shape[0]
    cell_count = score_bias.shape[1]
    hidden_width = proj_weight.shape[1]
    head_size = hidden_width // head_count
    scale_factor = head_size ** (-0.5)
    window_count = tile_x.shape[0]
    split_shape = (window_count, cell_count, head_count, head_size)
    joined_shape = (window_count, cell_count, hidden_width)
    x_float = tile_x.astype(jnp.float32)
    centred = x_float - lax.optimization_barrier(jnp.mean(x_float, -1, keepdims=True))
    inverse = lax.rsqrt(lax.optimization_barrier(jnp.mean(centred * centred, -1, keepdims=True)) + epsilon)
    normed = centred * inverse
    normed_low = normed.astype(jnp.bfloat16)
    mixed = jnp.einsum('wnc,ce->wne', normed_low.astype(jnp.float32), qkv_weight.astype(jnp.float32))
    query = (mixed[..., :hidden_width] * scale_factor).astype(jnp.bfloat16).reshape(split_shape)
    keys_low = mixed[..., hidden_width:2 * hidden_width].astype(jnp.bfloat16).reshape(split_shape)
    values_low = mixed[..., 2 * hidden_width:].astype(jnp.bfloat16).reshape(split_shape)
    scores = jnp.einsum('wqhd,wkhd->whqk', query.astype(jnp.float32), keys_low.astype(jnp.float32)) + score_bias[None]
    open_keys = (wet_cells > 0)[:, None, None, :]
    scores = jnp.where(open_keys, scores, -jnp.inf)
    raised = jnp.exp(scores - lax.optimization_barrier(jnp.max(scores, -1, keepdims=True)))
    probs = raised / lax.optimization_barrier(jnp.sum(raised, -1, keepdims=True))
    probs_low = probs.astype(jnp.bfloat16)
    attended = jnp.einsum('whqk,wkhd->wqhd', probs_low.astype(jnp.float32), values_low.astype(jnp.float32))
    attended = attended.reshape(joined_shape).astype(jnp.bfloat16)
    branch = jnp.einsum('wne,ce->wnc', attended.astype(jnp.float32), proj_weight.astype(jnp.float32))
    mask_rows = live_rows[:, None, None]
    windows_out = ((x_float + branch) * mask_rows).astype(jnp.bfloat16)
    grad_live = jnp.where(mask_rows > 0, tile_g, jnp.zeros_like(tile_g))
    grad_float = grad_live.astype(jnp.float32)
    proj_grad = jnp.einsum('wnc,wne->ce', grad_float, attended.astype(jnp.float32))
    attended_grad = jnp.einsum('wnc,ce->wne', grad_float, proj_weight.astype(jnp.float32))
    attended_grad = attended_grad.astype(jnp.bfloat16).reshape(split_shape).astype(jnp.float32)
    probs_grad = jnp.einsum('wqhd,wkhd->whqk', attended_grad, values_low.astype(jnp.float32))
    values_grad = jnp.einsum('whqk,wqhd->wkhd', probs_low.astype(jnp.float32), attended_grad)
    score_grad = probs * (probs_grad - lax.optimization_barrier(jnp.sum(probs * probs_grad, -1, keepdims=True)))
    score_grad = score_grad.astype(jnp.bfloat16).astype(jnp.float32)
    query_grad = jnp.einsum('whqk,wkhd->wqhd', score_grad, keys_low.astype(jnp.float32)) * scale_factor
    keys_grad = jnp.einsum('whqk,wqhd->wkhd', score_grad, query.astype(jnp.float32))
    mixed_grad = jnp.concatenate([query_grad.reshape(joined_shape), keys_grad.reshape(joined_shape), values_grad.reshape(joined_shape)], -1)
    mixed_grad = mixed_grad.astype(jnp.bfloat16).astype(jnp.float32)
    normed_grad = jnp.einsum('wne,ce->wnc', mixed_grad, qkv_weight.astype(jnp.float32))
    branch_grad = inverse * (normed_grad - lax.optimization_barrier(jnp.mean(normed_grad, -1, keepdims=True)) - normed * lax.optimization_barrier(jnp.mean(normed_grad * normed, -1, keepdims=True)))
    input_grad = (grad_float + branch_grad).astype(jnp.bfloat16)
    return (windows_out, input_grad, proj_grad)

def reference(windows_in, cotangent, wet_mask, wet_count, qkv_weight, proj_weight, score_bias):
    window_ids = jnp.arange(WINDOWS, dtype=jnp.int32)
    slot_ids = window_ids % WIN_DEV
    tile_ids = window_ids // WIN_DEV

    def per_sample(running, sample):
        sample_x, sample_g, sample_wet, sample_count = sample
        live_rows = (slot_ids < sample_count[tile_ids]).astype(jnp.float32)
        result, grads_in, proj_part = window_pass(sample_x, sample_g, sample_wet, live_rows, qkv_weight, proj_weight, score_bias)
        return (running + proj_part, (result, grads_in))
    initial = jnp.zeros((C, HD), jnp.float32)
    total, outputs = lax.scan(per_sample, initial, (windows_in, cotangent, wet_mask, wet_count))
    return (outputs[0], outputs[1], total.reshape(-1))
```

```python
import functools
import jax
import jax.numpy as jnp
from jax import lax
from jax.experimental import pallas as pl
from jax.experimental.pallas import tpu as pltpu
from jax.sharding import PartitionSpec as P

EPSILON = 1e-05
PAIR = 128
VMEM_BYTES = 58 * 1024 * 1024
BF16 = jnp.bfloat16
F32 = jnp.float32


def dot(lhs, rhs, lhs_axis, rhs_axis):
    return lax.dot_general(
        lhs, rhs, (((lhs_axis,), (rhs_axis,)), ((), ())), preferred_element_type=F32
    )


def make_spread(cells, size):
    same_head = (
        lax.broadcasted_iota(jnp.int32, (PAIR, PAIR), 0) // size
        == lax.broadcasted_iota(jnp.int32, (PAIR, PAIR), 1) // size
    )
    first_head = lax.broadcasted_iota(jnp.int32, (cells, PAIR), 1) < size

    def spread(low):
        return jnp.where(same_head, jnp.concatenate([low, low], 0), jnp.zeros((), BF16))

    def own(both):
        return jnp.where(first_head, both[:cells], both[cells:])

    return spread, own


def keep_live(ref, count_ref, cells):
    live = lax.broadcasted_iota(jnp.int32, (ref.shape[0], 1), 0) < count_ref[0, 0] * cells
    ref[...] = jnp.where(live, ref[...], jnp.zeros((), BF16))


class Fetch:
    def __init__(self, sems):
        self.sems = sems
        self.used = 0

    def __call__(self, source, target):
        copy = pltpu.make_async_copy(source, target, self.sems.at[self.used])
        self.used += 1
        copy.start()
        return copy


def attend(
    wet_ref, bias_ref, x_ref, qkv_ref, mixed_ref, attended_ref, probs_ref, probs_low_ref, scores_ref, bias_t_ref,
    normed_ref, inverse_ref, x_wait, small_waits, qkv_wait, sizes,
):
    windows, cells, heads = sizes
    hidden = attended_ref.shape[1]
    size = hidden // heads
    pairs = hidden // PAIR
    scale = size ** (-0.5)
    spread, own = make_spread(cells, size)

    x_wait()
    x_float = x_ref[...].astype(F32)
    centred = x_float - jnp.mean(x_float, -1, keepdims=True)
    inverse = lax.rsqrt(jnp.mean(centred * centred, -1, keepdims=True) + EPSILON)
    normed = centred * inverse
    if normed_ref is not None:
        normed_ref[...] = normed
        inverse_ref[...] = inverse
    normed_low = normed.astype(BF16)
    small_waits()
    bias_t_ref[...] = bias_ref[...].T
    closed = jnp.where(wet_ref[...] > 0, 0.0, -jnp.inf).astype(F32).T
    qkv_wait()
    for part in range(3):
        lanes = slice(part * hidden, (part + 1) * hidden)
        mixed = dot(normed_low, qkv_ref[:, lanes], 1, 0)
        if part == 0:
            mixed = mixed * scale
        mixed_ref[:, lanes] = mixed.astype(BF16)

    for window in range(windows):
        at = slice(window * cells, (window + 1) * cells)
        for pair in range(pairs):
            lanes = slice(pair * PAIR, (pair + 1) * PAIR)
            query = mixed_ref[at, lanes]
            keys = mixed_ref[at, hidden + pair * PAIR : hidden + (pair + 1) * PAIR]
            scores = dot(keys, spread(query), 1, 1) + bias_t_ref[:, lanes]
            scores_ref[at, lanes] = scores + closed[:, window : window + 1]
    for window in range(windows):
        at = slice(window * cells, (window + 1) * cells)
        scores = scores_ref[at, :]
        raised = jnp.exp(scores - jnp.max(scores, 0, keepdims=True))
        probs = raised * (1.0 / jnp.sum(raised, 0, keepdims=True))
        probs_low_ref[at, :] = probs.astype(BF16)
        if probs_ref is not None:
            probs_ref[at, :] = probs
    for window in range(windows):
        at = slice(window * cells, (window + 1) * cells)
        for pair in range(pairs):
            lanes = slice(pair * PAIR, (pair + 1) * PAIR)
            values = mixed_ref[at, 2 * hidden + pair * PAIR : 2 * hidden + (pair + 1) * PAIR]
            attended_ref[at, lanes] = own(dot(probs_low_ref[at, lanes], values, 0, 0)).astype(BF16)


def share_kernel(
    wet_hbm, bias_hbm, count_ref, x_hbm, g_hbm, qkv_hbm, share_ref,
    wet_ref, bias_ref, x_ref, g_ref, qkv_ref, mixed_ref, attended_ref, bias_t_ref, probs_low_ref, scores_ref,
    lines_ref, sems, *, sizes, outer, inner,
):
    rows, width = x_ref.shape
    cells = sizes[1]
    pairs = attended_ref.shape[1] // PAIR
    fetch = Fetch(sems)
    x_copy = fetch(x_hbm, x_ref)
    bias_copy = fetch(bias_hbm, bias_ref)
    wet_copy = fetch(wet_hbm, wet_ref)
    qkv_copy = fetch(qkv_hbm, qkv_ref)
    g_copy = fetch(g_hbm, g_ref)

    def small_waits():
        bias_copy.wait()
        wet_copy.wait()

    attend(
        wet_ref, bias_ref, x_ref, qkv_ref, mixed_ref, attended_ref, None, probs_low_ref, scores_ref, bias_t_ref,
        None, None, x_copy.wait, small_waits, qkv_copy.wait, sizes,
    )
    g_copy.wait()
    keep_live(g_ref, count_ref, cells)
    total = dot(g_ref[...], attended_ref[...], 0, 0)
    for k in range(pairs):
        part = total[:, k * PAIR : (k + 1) * PAIR].reshape(outer, inner, PAIR)
        part = jnp.transpose(part, (1, 0, 2)).reshape(inner // 2, 2, outer, PAIR)
        for core in range(2):
            lines = pl.ds(core * width * pairs // 2 + k, width // 2, stride=pairs)
            lines_ref[lines, :] = part[:, core].reshape(width // 2, PAIR)
    share_ref[...] = lines_ref[...].astype(BF16).reshape(share_ref.shape)


def grads_kernel(
    wet_hbm, bias_hbm, count_ref, x_hbm, g_hbm, qkv_hbm, proj_hbm, out_hbm, grad_hbm,
    wet_ref, bias_ref, x_ref, g_ref, qkv_ref, proj_ref, mixed_ref, attended_ref, bias_t_ref, probs_low_ref, scores_ref,
    probs_ref, normed_ref, inverse_ref, agrad_ref, mgrad_ref, out_ref, grad_ref,
    sems, *, sizes,
):
    windows, cells, heads = sizes
    rows, width = x_ref.shape
    hidden = proj_ref.shape[1]
    size = hidden // heads
    pairs = hidden // PAIR
    scale = size ** (-0.5)
    spread, own = make_spread(cells, size)
    fetch = Fetch(sems)
    x_copy = fetch(x_hbm, x_ref)
    bias_copy = fetch(bias_hbm, bias_ref)
    wet_copy = fetch(wet_hbm, wet_ref)
    qkv_copy = fetch(qkv_hbm, qkv_ref)
    g_copy = fetch(g_hbm, g_ref)
    proj_copy = fetch(proj_hbm, proj_ref)

    def small_waits():
        bias_copy.wait()
        wet_copy.wait()

    attend(
        wet_ref, bias_ref, x_ref, qkv_ref, mixed_ref, attended_ref, probs_ref, probs_low_ref, scores_ref, bias_t_ref,
        normed_ref, inverse_ref, x_copy.wait, small_waits, qkv_copy.wait, sizes,
    )
    g_copy.wait()
    keep_live(g_ref, count_ref, cells)
    proj_copy.wait()
    branch = dot(attended_ref[...], proj_ref[...], 1, 1)
    out_ref[...] = (x_ref[...].astype(F32) + branch).astype(BF16)
    keep_live(out_ref, count_ref, cells)
    out_copy = fetch(out_ref, out_hbm)
    agrad_ref[...] = dot(g_ref[...], proj_ref[...], 1, 0).astype(BF16)

    for window in range(windows):
        at = slice(window * cells, (window + 1) * cells)
        for pair in range(pairs):
            lanes = slice(pair * PAIR, (pair + 1) * PAIR)
            value_lanes = slice(2 * hidden + pair * PAIR, 2 * hidden + (pair + 1) * PAIR)
            agrad = spread(agrad_ref[at, lanes])
            scores_ref[at, lanes] = dot(mixed_ref[at, value_lanes], agrad, 1, 1)
            mgrad_ref[at, value_lanes] = dot(probs_low_ref[at, lanes], agrad, 1, 0).astype(BF16)
    for window in range(windows):
        at = slice(window * cells, (window + 1) * cells)
        probs = probs_ref[at, :]
        probs_grad = scores_ref[at, :]
        score_grad = probs * (probs_grad - jnp.sum(probs * probs_grad, 0, keepdims=True))
        probs_low_ref[at, :] = score_grad.astype(BF16)
    for window in range(windows):
        at = slice(window * cells, (window + 1) * cells)
        for pair in range(pairs):
            lanes = slice(pair * PAIR, (pair + 1) * PAIR)
            key_lanes = slice(hidden + pair * PAIR, hidden + (pair + 1) * PAIR)
            score_grad = probs_low_ref[at, lanes]
            query_grad = own(dot(score_grad, mixed_ref[at, key_lanes], 0, 0)) * scale
            mgrad_ref[at, lanes] = query_grad.astype(BF16)
            keys_grad = dot(score_grad, spread(mixed_ref[at, lanes]), 1, 0)
            mgrad_ref[at, key_lanes] = keys_grad.astype(BF16)

    normed_grad = dot(mgrad_ref[...], qkv_ref[...], 1, 1)
    normed = normed_ref[...]
    branch_grad = inverse_ref[...] * (
        normed_grad
        - jnp.mean(normed_grad, -1, keepdims=True)
        - normed * jnp.mean(normed_grad * normed, -1, keepdims=True)
    )
    grad_ref[...] = (g_ref[...].astype(F32) + branch_grad).astype(BF16)
    grad_copy = fetch(grad_ref, grad_hbm)
    out_copy.wait()
    grad_copy.wait()


def staging(x, g, wet, count, qkv_weight, score_bias):
    windows, cells, width = x.shape
    heads = score_bias.shape[0]
    hidden = qkv_weight.shape[1] // 3
    rows = windows * cells
    staged = [
        pltpu.VMEM((windows, cells), jnp.int32),
        pltpu.VMEM((heads * cells, cells), F32),
        pltpu.VMEM((rows, width), BF16),
        pltpu.VMEM((rows, width), BF16),
        pltpu.VMEM((width, 3 * hidden), BF16),
    ]
    worked = [
        pltpu.VMEM((rows, 3 * hidden), BF16),
        pltpu.VMEM((rows, hidden), BF16),
        pltpu.VMEM((cells, hidden), F32),
        pltpu.VMEM((rows, hidden), BF16),
        pltpu.VMEM((rows, hidden), F32),
    ]
    args = (
        wet,
        score_bias.reshape(heads * cells, cells),
        count,
        x.reshape(rows, width),
        g.reshape(rows, width),
        qkv_weight,
    )
    return args, staged, worked, (windows, cells, heads)


def placed(arrays):
    specs = [pl.BlockSpec(memory_space=pltpu.HBM)] * arrays
    return specs[:2] + [pl.BlockSpec(memory_space=pltpu.SMEM)] + specs[2:]


def share_call(x, g, wet, count, qkv_weight, score_bias, outer, inner):
    args, staged, worked, sizes = staging(x, g, wet, count, qkv_weight, score_bias)
    rows, width = args[3].shape
    hidden = qkv_weight.shape[1] // 3
    pairs = hidden // PAIR
    return pl.pallas_call(
        functools.partial(share_kernel, sizes=sizes, outer=outer, inner=inner),
        out_shape=jax.ShapeDtypeStruct((2, inner // 2, outer * pairs, PAIR), BF16),
        in_specs=placed(5),
        out_specs=pl.BlockSpec(memory_space=pltpu.VMEM),
        scratch_shapes=staged
        + worked
        + [
            pltpu.VMEM((width * pairs, PAIR), F32),
            pltpu.SemaphoreType.DMA((5,)),
        ],
        compiler_params=pltpu.CompilerParams(vmem_limit_bytes=VMEM_BYTES),
        cost_estimate=pl.CostEstimate(
            flops=2 * rows * width * 4 * hidden, bytes_accessed=4_000_000, transcendentals=200_000
        ),
    )(*args)


def grads_call(x, g, wet, count, qkv_weight, proj_weight, score_bias):
    args, staged, worked, sizes = staging(x, g, wet, count, qkv_weight, score_bias)
    rows, width = args[3].shape
    hidden = proj_weight.shape[1]
    hbm = pl.BlockSpec(memory_space=pltpu.HBM)
    flat = jax.ShapeDtypeStruct((rows, width), BF16)
    return pl.pallas_call(
        functools.partial(grads_kernel, sizes=sizes),
        out_shape=(flat, flat),
        in_specs=placed(6),
        out_specs=(hbm, hbm),
        scratch_shapes=staged
        + [pltpu.VMEM((width, hidden), BF16)]
        + worked
        + [
            pltpu.VMEM((rows, hidden), F32),
            pltpu.VMEM((rows, width), F32),
            pltpu.VMEM((rows, 1), F32),
            pltpu.VMEM((rows, hidden), BF16),
            pltpu.VMEM((rows, 3 * hidden), BF16),
            pltpu.VMEM((rows, width), BF16),
            pltpu.VMEM((rows, width), BF16),
            pltpu.SemaphoreType.DMA((8,)),
        ],
        compiler_params=pltpu.CompilerParams(vmem_limit_bytes=VMEM_BYTES),
        cost_estimate=pl.CostEstimate(
            flops=2 * rows * width * 16 * hidden, bytes_accessed=30_000_000, transcendentals=200_000
        ),
    )(*args, proj_weight)


def block_call(x, g, wet, count, qkv_weight, proj_weight, score_bias, outer, inner):
    share = share_call(x, g, wet, count, qkv_weight, score_bias, outer, inner)
    out, grad = grads_call(x, g, wet, count, qkv_weight, proj_weight, score_bias)
    return out, grad, share


def shards(windows_in, cotangent, wet_mask, wet_count, qkv_weight, proj_weight, score_bias):
    outer, inner = lax.axis_size("space"), lax.axis_size("dp")
    pairs = proj_weight.shape[1] // PAIR
    x, g = windows_in[0], cotangent[0]
    wet, count = wet_mask[0], wet_count
    share = share_call(x, g, wet, count, qkv_weight, score_bias, outer, inner)
    pairs_of_cores = [(i, i ^ 1) for i in range(inner)]
    core = lax.rem(lax.axis_index("dp"), 2)
    sent = lax.dynamic_index_in_dim(share, 1 - core, 0, keepdims=False)
    held = lax.dynamic_index_in_dim(share, core, 0, keepdims=False)
    got = lax.ppermute(sent, "dp", pairs_of_cores)
    share = (held.astype(F32) + got.astype(F32)).astype(BF16)
    wet, share = lax.optimization_barrier((wet, share))
    groups = [list(range(core, inner, 2)) for core in range(2)]
    got = lax.all_to_all(share, "dp", 0, 0, tiled=True, axis_index_groups=groups)
    out, grad = grads_call(x, g, wet, count, qkv_weight, proj_weight, score_bias)
    got, out, grad = lax.optimization_barrier((got, out, grad))
    part = jnp.sum(got.astype(F32), 0).astype(BF16).reshape(outer, pairs, PAIR)
    got = lax.all_to_all(part, "space", 0, 0, tiled=True)
    total = jnp.sum(got.astype(F32), 0).reshape(-1)
    return (out.reshape(windows_in.shape), grad.reshape(windows_in.shape), total)


def solution(mesh):
    in_specs = (
        P("dp", "space", None, None),
        P("dp", "space", None, None),
        P("dp", "space", None),
        P("dp", "space"),
        P(),
        P(),
        P(),
    )
    out_specs = (P("dp", "space", None, None), P("dp", "space", None, None), P(("space", "dp")))
    return jax.shard_map(shards, mesh=mesh, in_specs=in_specs, out_specs=out_specs, check_vma=False)
```

```python
import functools
import jax
import jax.numpy as jnp
from jax import lax
from jax.experimental import pallas as pl
from jax.experimental.pallas import tpu as pltpu
from jax.sharding import Mesh, PartitionSpec as P

EPSILON = 1e-05
PAIR = 128
AXES = ("z", "xlo", "xhi", "y", "core")
OUTER = ("z", "xlo")
INNER = ("xhi", "y")
VMEM_BYTES = 32 * 1024 * 1024
BF16 = jnp.bfloat16
F32 = jnp.float32


def dot(lhs, rhs, lhs_axis, rhs_axis):
    return lax.dot_general(
        lhs, rhs, (((lhs_axis,), (rhs_axis,)), ((), ())), preferred_element_type=F32
    )


def make_spread(cells, size):
    same_head = (
        lax.broadcasted_iota(jnp.int32, (PAIR, PAIR), 0) // size
        == lax.broadcasted_iota(jnp.int32, (PAIR, PAIR), 1) // size
    )
    first_head = lax.broadcasted_iota(jnp.int32, (cells, PAIR), 1) < size

    def spread(low):
        return jnp.where(same_head, jnp.concatenate([low, low], 0), jnp.zeros((), BF16))

    def own(both):
        return jnp.where(first_head, both[:cells], both[cells:])

    return spread, own


def keep_live(ref, count_ref, cells):
    live = lax.broadcasted_iota(jnp.int32, (ref.shape[0], 1), 0) < count_ref[0, 0] * cells
    ref[...] = jnp.where(live, ref[...], jnp.zeros((), BF16))


class Fetch:
    def __init__(self, sems):
        self.sems = sems
        self.used = 0

    def __call__(self, source, target):
        copy = pltpu.make_async_copy(source, target, self.sems.at[self.used])
        self.used += 1
        copy.start()
        return copy


def attend(
    wet_ref, bias_ref, x_ref, qkv_ref, mixed_ref, attended_ref, probs_ref, probs_low_ref, scores_ref, bias_t_ref,
    normed_ref, inverse_ref, x_wait, small_waits, qkv_wait, sizes, between=None,
):
    windows, cells, heads = sizes
    hidden = attended_ref.shape[1]
    size = hidden // heads
    pairs = hidden // PAIR
    scale = size ** (-0.5)
    spread, own = make_spread(cells, size)

    x_wait()
    small_waits()
    bias_t_ref[...] = bias_ref[...].T
    closed = jnp.where(wet_ref[...] > 0, 0.0, -jnp.inf).astype(F32).T
    step = x_ref.shape[0] // 2
    lows = []
    for part in range(2):
        at = slice(part * step, (part + 1) * step)
        x_float = x_ref[at, :].astype(F32)
        centred = x_float - jnp.mean(x_float, -1, keepdims=True)
        inverse = lax.rsqrt(jnp.mean(centred * centred, -1, keepdims=True) + EPSILON)
        normed = centred * inverse
        if normed_ref is not None:
            normed_ref[at, :] = normed
            inverse_ref[at, :] = inverse
        lows.append(normed.astype(BF16))
    qkv_wait()
    for part in range(2):
        at = slice(part * step, (part + 1) * step)
        mixed = dot(lows[part], qkv_ref[...], 1, 0)
        mixed_ref[at, :hidden] = (mixed[:, :hidden] * scale).astype(BF16)
        mixed_ref[at, hidden:] = mixed[:, hidden:].astype(BF16)

    if between is not None:
        between()
    for window in range(windows):
        at = slice(window * cells, (window + 1) * cells)
        for pair in range(pairs):
            lanes = slice(pair * PAIR, (pair + 1) * PAIR)
            query = mixed_ref[at, lanes]
            keys = mixed_ref[at, hidden + pair * PAIR : hidden + (pair + 1) * PAIR]
            scores = dot(keys, spread(query), 1, 1) + bias_t_ref[:, lanes]
            scores_ref[at, lanes] = scores + closed[:, window : window + 1]
    for window in range(windows):
        at = slice(window * cells, (window + 1) * cells)
        scores = scores_ref[at, :]
        raised = jnp.exp(scores - jnp.max(scores, 0, keepdims=True))
        probs = raised * (1.0 / jnp.sum(raised, 0, keepdims=True))
        probs_low_ref[at, :] = probs.astype(BF16)
        if probs_ref is not None:
            probs_ref[at, :] = probs
    for window in range(windows):
        at = slice(window * cells, (window + 1) * cells)
        for pair in range(pairs):
            lanes = slice(pair * PAIR, (pair + 1) * PAIR)
            values = mixed_ref[at, 2 * hidden + pair * PAIR : 2 * hidden + (pair + 1) * PAIR]
            attended_ref[at, lanes] = own(dot(probs_low_ref[at, lanes], values, 0, 0)).astype(BF16)


def share_kernel(
    wet_hbm, bias_hbm, count_ref, x_hbm, g_hbm, qkv_hbm, held_ref, sent_ref,
    wet_ref, bias_ref, x_ref, g_ref, qkv_ref, mixed_ref, attended_ref, bias_t_ref, probs_low_ref, scores_ref,
    turned_ref, lines_ref, sems, *, sizes, outer, inner,
):
    rows, width = x_ref.shape
    cells = sizes[1]
    pairs = attended_ref.shape[1] // PAIR
    fetch = Fetch(sems)
    x_copy = fetch(x_hbm, x_ref)
    bias_copy = fetch(bias_hbm, bias_ref)
    wet_copy = fetch(wet_hbm, wet_ref)
    qkv_copy = fetch(qkv_hbm, qkv_ref)
    g_copy = fetch(g_hbm, g_ref)

    def small_waits():
        bias_copy.wait()
        wet_copy.wait()

    def turn():
        g_copy.wait()
        keep_live(g_ref, count_ref, cells)
        turned_ref[...] = g_ref[...].T

    attend(
        wet_ref, bias_ref, x_ref, qkv_ref, mixed_ref, attended_ref, None, probs_low_ref, scores_ref, bias_t_ref,
        None, None, x_copy.wait, small_waits, qkv_copy.wait, sizes, turn,
    )
    total = dot(turned_ref[...], attended_ref[...], 1, 0)
    half = width // 2
    for k in range(pairs):
        part = total[:, k * PAIR : (k + 1) * PAIR].reshape(outer, 2 * inner, PAIR)
        part = jnp.transpose(part, (1, 0, 2)).reshape(inner, 2, outer, PAIR)
        for core in range(2):
            lines = pl.ds(core * half * pairs + k, half, stride=pairs)
            lines_ref[lines, :] = part[:, core].reshape(half, PAIR)
    core = lax.axis_index("core")
    held = pl.ds(pl.multiple_of(core * half * pairs, half * pairs), half * pairs)
    sent = pl.ds(pl.multiple_of((1 - core) * half * pairs, half * pairs), half * pairs)
    held_ref[...] = lines_ref[held, :].astype(held_ref.dtype).reshape(held_ref.shape)
    sent_ref[...] = lines_ref[sent, :].astype(sent_ref.dtype).reshape(sent_ref.shape)


def grads_kernel(
    wet_hbm, bias_hbm, count_ref, x_hbm, g_hbm, qkv_hbm, proj_hbm, out_hbm, grad_hbm,
    wet_ref, bias_ref, x_ref, g_ref, qkv_ref, proj_ref, mixed_ref, attended_ref, bias_t_ref, probs_low_ref, scores_ref,
    probs_ref, normed_ref, inverse_ref, agrad_ref, mgrad_ref, out_ref, grad_ref,
    sems, *, sizes,
):
    windows, cells, heads = sizes
    rows, width = x_ref.shape
    hidden = proj_ref.shape[1]
    size = hidden // heads
    pairs = hidden // PAIR
    scale = size ** (-0.5)
    spread, own = make_spread(cells, size)
    fetch = Fetch(sems)
    x_copy = fetch(x_hbm, x_ref)
    bias_copy = fetch(bias_hbm, bias_ref)
    wet_copy = fetch(wet_hbm, wet_ref)
    qkv_copy = fetch(qkv_hbm, qkv_ref)
    g_copy = fetch(g_hbm, g_ref)
    proj_copy = fetch(proj_hbm, proj_ref)

    def small_waits():
        bias_copy.wait()
        wet_copy.wait()

    attend(
        wet_ref, bias_ref, x_ref, qkv_ref, mixed_ref, attended_ref, probs_ref, probs_low_ref, scores_ref, bias_t_ref,
        normed_ref, inverse_ref, x_copy.wait, small_waits, qkv_copy.wait, sizes,
    )
    g_copy.wait()
    keep_live(g_ref, count_ref, cells)
    proj_copy.wait()
    branch = dot(attended_ref[...], proj_ref[...], 1, 1)
    out_ref[...] = (x_ref[...].astype(F32) + branch).astype(BF16)
    keep_live(out_ref, count_ref, cells)
    out_copy = fetch(out_ref, out_hbm)
    agrad_ref[...] = dot(g_ref[...], proj_ref[...], 1, 0).astype(BF16)

    for window in range(windows):
        at = slice(window * cells, (window + 1) * cells)
        for pair in range(pairs):
            lanes = slice(pair * PAIR, (pair + 1) * PAIR)
            value_lanes = slice(2 * hidden + pair * PAIR, 2 * hidden + (pair + 1) * PAIR)
            agrad = spread(agrad_ref[at, lanes])
            scores_ref[at, lanes] = dot(mixed_ref[at, value_lanes], agrad, 1, 1)
            mgrad_ref[at, value_lanes] = dot(probs_low_ref[at, lanes], agrad, 1, 0).astype(BF16)
    for window in range(windows):
        at = slice(window * cells, (window + 1) * cells)
        probs = probs_ref[at, :]
        probs_grad = scores_ref[at, :]
        score_grad = probs * (probs_grad - jnp.sum(probs * probs_grad, 0, keepdims=True))
        probs_low_ref[at, :] = score_grad.astype(BF16)
    for window in range(windows):
        at = slice(window * cells, (window + 1) * cells)
        for pair in range(pairs):
            lanes = slice(pair * PAIR, (pair + 1) * PAIR)
            key_lanes = slice(hidden + pair * PAIR, hidden + (pair + 1) * PAIR)
            score_grad = probs_low_ref[at, lanes]
            query_grad = own(dot(score_grad, mixed_ref[at, key_lanes], 0, 0)) * scale
            mgrad_ref[at, lanes] = query_grad.astype(BF16)
            keys_grad = dot(score_grad, spread(mixed_ref[at, lanes]), 1, 0)
            mgrad_ref[at, key_lanes] = keys_grad.astype(BF16)

    normed_grad = dot(mgrad_ref[...], qkv_ref[...], 1, 1)
    normed = normed_ref[...]
    branch_grad = inverse_ref[...] * (
        normed_grad
        - jnp.mean(normed_grad, -1, keepdims=True)
        - normed * jnp.mean(normed_grad * normed, -1, keepdims=True)
    )
    grad_ref[...] = (g_ref[...].astype(F32) + branch_grad).astype(BF16)
    grad_copy = fetch(grad_ref, grad_hbm)
    out_copy.wait()
    grad_copy.wait()


def staging(x, g, wet, count, qkv_weight, score_bias):
    windows, cells, width = x.shape
    heads = score_bias.shape[0]
    hidden = qkv_weight.shape[1] // 3
    rows = windows * cells
    staged = [
        pltpu.VMEM((windows, cells), jnp.int32),
        pltpu.VMEM((heads * cells, cells), F32),
        pltpu.VMEM((rows, width), BF16),
        pltpu.VMEM((rows, width), BF16),
        pltpu.VMEM((width, 3 * hidden), BF16),
    ]
    worked = [
        pltpu.VMEM((rows, 3 * hidden), BF16),
        pltpu.VMEM((rows, hidden), BF16),
        pltpu.VMEM((cells, hidden), F32),
        pltpu.VMEM((rows, hidden), BF16),
        pltpu.VMEM((rows, hidden), F32),
    ]
    args = (
        wet,
        score_bias.reshape(heads * cells, cells),
        count,
        x.reshape(rows, width),
        g.reshape(rows, width),
        qkv_weight,
    )
    return args, staged, worked, (windows, cells, heads)


def placed(arrays):
    specs = [pl.BlockSpec(memory_space=pltpu.HBM)] * arrays
    return specs[:2] + [pl.BlockSpec(memory_space=pltpu.SMEM)] + specs[2:]


def pinned(args):
    return [
        arg if arg.size == 1 else pltpu.with_memory_space_constraint(arg, pltpu.HBM)
        for arg in args
    ]


def share_call(x, g, wet, count, qkv_weight, score_bias, outer, inner):
    args, staged, worked, sizes = staging(x, g, wet, count, qkv_weight, score_bias)
    rows, width = args[3].shape
    hidden = qkv_weight.shape[1] // 3
    pairs = hidden // PAIR
    return pl.pallas_call(
        functools.partial(share_kernel, sizes=sizes, outer=outer, inner=inner),
        out_shape=(
            pltpu.VMEM((inner, outer * pairs, PAIR), F32),
            pltpu.VMEM((inner, outer * pairs, PAIR), BF16),
        ),
        in_specs=placed(5),
        out_specs=[pl.BlockSpec(memory_space=pltpu.VMEM)] * 2,
        scratch_shapes=staged
        + worked
        + [
            pltpu.VMEM((width, rows), BF16),
            pltpu.VMEM((width * pairs, PAIR), F32),
            pltpu.SemaphoreType.DMA((5,)),
        ],
        compiler_params=pltpu.CompilerParams(vmem_limit_bytes=VMEM_BYTES),
        cost_estimate=pl.CostEstimate(
            flops=2 * rows * width * 4 * hidden, bytes_accessed=4_000_000, transcendentals=200_000
        ),
    )(*pinned(args))


def grads_call(x, g, wet, count, qkv_weight, proj_weight, score_bias):
    args, staged, worked, sizes = staging(x, g, wet, count, qkv_weight, score_bias)
    rows, width = args[3].shape
    hidden = proj_weight.shape[1]
    hbm = pl.BlockSpec(memory_space=pltpu.HBM)
    flat = jax.ShapeDtypeStruct((rows, width), BF16)
    return pl.pallas_call(
        functools.partial(grads_kernel, sizes=sizes),
        out_shape=(flat, flat),
        in_specs=placed(6),
        out_specs=(hbm, hbm),
        scratch_shapes=staged
        + [pltpu.VMEM((width, hidden), BF16)]
        + worked
        + [
            pltpu.VMEM((rows, hidden), F32),
            pltpu.VMEM((rows, width), F32),
            pltpu.VMEM((rows, 1), F32),
            pltpu.VMEM((rows, hidden), BF16),
            pltpu.VMEM((rows, 3 * hidden), BF16),
            pltpu.VMEM((rows, width), BF16),
            pltpu.VMEM((rows, width), BF16),
            pltpu.SemaphoreType.DMA((8,)),
        ],
        compiler_params=pltpu.CompilerParams(vmem_limit_bytes=VMEM_BYTES),
        cost_estimate=pl.CostEstimate(
            flops=2 * rows * width * 16 * hidden, bytes_accessed=30_000_000, transcendentals=200_000
        ),
    )(*pinned(args + (proj_weight,)))


def block_call(x, g, wet, count, qkv_weight, proj_weight, score_bias, outer, inner):
    share = share_call(x, g, wet, count, qkv_weight, score_bias, outer, inner)
    out, grad = grads_call(x, g, wet, count, qkv_weight, proj_weight, score_bias)
    return out, grad, share


def shards(windows_in, cotangent, wet, count, qkv_weight, proj_weight, score_bias):
    outer, inner = lax.axis_size(OUTER), lax.axis_size(INNER)
    pairs = proj_weight.shape[1] // PAIR
    x, g, wet = windows_in[0], cotangent[0], wet[0]
    held, sent = share_call(x, g, wet, count, qkv_weight, score_bias, outer, inner)
    got = lax.ppermute(sent, "core", [(0, 1), (1, 0)])
    share = (held + got.astype(F32)).astype(BF16)
    wet, share = lax.optimization_barrier((wet, share))
    got = lax.all_to_all(share, INNER, 0, 0, tiled=True)
    out, grad = grads_call(x, g, wet, count, qkv_weight, proj_weight, score_bias)
    got, out, grad = lax.optimization_barrier((got, out, grad))
    part = jnp.sum(got.astype(F32), 0).reshape(outer, pairs, PAIR)
    got = lax.all_to_all(part, OUTER, 0, 0, tiled=True)
    total = jnp.sum(got, 0).reshape(-1)
    return (out.reshape(windows_in.shape), grad.reshape(windows_in.shape), total)


def solution(mesh):
    space, dp = mesh.devices.shape
    split = Mesh(mesh.devices.reshape(space // 2, 2, 2, dp // 4, 2), AXES)
    tiles, samples = ("z", "xlo"), ("xhi", "y", "core")
    in_specs = (
        P(samples, tiles, None, None),
        P(samples, tiles, None, None),
        P(samples, tiles, None),
        P(samples, tiles),
        P(),
        P(),
        P(),
    )
    out_specs = (P(samples, tiles, None, None), P(samples, tiles, None, None), P(AXES))
    return jax.shard_map(shards, mesh=split, in_specs=in_specs, out_specs=out_specs, check_vma=False)
```

```python
import functools
import jax
import jax.numpy as jnp
from jax import lax
from jax.experimental import pallas as pl
from jax.experimental.pallas import tpu as pltpu
from jax.sharding import PartitionSpec as P

EPSILON = 1e-05
PAIR = 128
FIRST_OUTER = 19
FIRST_INNER = 13
VMEM_BYTES = 32 * 1024 * 1024
BF16 = jnp.bfloat16
F32 = jnp.float32


def dot(lhs, rhs, lhs_axis, rhs_axis):
    return lax.dot_general(
        lhs, rhs, (((lhs_axis,), (rhs_axis,)), ((), ())), preferred_element_type=F32
    )


def make_spread(cells, size):
    same_head = (
        lax.broadcasted_iota(jnp.int32, (PAIR, PAIR), 0) // size
        == lax.broadcasted_iota(jnp.int32, (PAIR, PAIR), 1) // size
    )
    first_head = lax.broadcasted_iota(jnp.int32, (cells, PAIR), 1) < size

    def spread(low):
        return jnp.where(same_head, jnp.concatenate([low, low], 0), jnp.zeros((), BF16))

    def own(both):
        return jnp.where(first_head, both[:cells], both[cells:])

    return spread, own


def turned_by(array, first):
    return jnp.concatenate([array[first:], array[:first]], 0)


def keep_live(ref, count_ref, cells):
    live = lax.broadcasted_iota(jnp.int32, (ref.shape[0], 1), 0) < count_ref[0, 0] * cells
    ref[...] = jnp.where(live, ref[...], jnp.zeros((), BF16))


class Fetch:
    def __init__(self, sems):
        self.sems = sems
        self.used = 0

    def __call__(self, source, target):
        copy = pltpu.make_async_copy(source, target, self.sems.at[self.used])
        self.used += 1
        copy.start()
        return copy


def attend(
    wet_ref, bias_ref, x_ref, qkv_ref, mixed_ref, attended_ref, probs_ref, probs_low_ref, scores_ref, bias_t_ref,
    normed_ref, inverse_ref, x_wait, small_waits, qkv_wait, sizes, between=None,
):
    windows, cells, heads = sizes
    hidden = attended_ref.shape[1]
    size = hidden // heads
    pairs = hidden // PAIR
    scale = size ** (-0.5)
    spread, own = make_spread(cells, size)

    x_wait()
    small_waits()
    bias_t_ref[...] = bias_ref[...].T
    closed = jnp.where(wet_ref[...] > 0, 0.0, -jnp.inf).astype(F32).T
    step = x_ref.shape[0] // 2
    lows = []
    for part in range(2):
        at = slice(part * step, (part + 1) * step)
        x_float = x_ref[at, :].astype(F32)
        centred = x_float - jnp.mean(x_float, -1, keepdims=True)
        inverse = lax.rsqrt(jnp.mean(centred * centred, -1, keepdims=True) + EPSILON)
        normed = centred * inverse
        if normed_ref is not None:
            normed_ref[at, :] = normed
            inverse_ref[at, :] = inverse
        lows.append(normed.astype(BF16))
    qkv_wait()
    for part in range(2):
        at = slice(part * step, (part + 1) * step)
        mixed = dot(lows[part], qkv_ref[...], 1, 0)
        mixed_ref[at, :hidden] = (mixed[:, :hidden] * scale).astype(BF16)
        mixed_ref[at, hidden:] = mixed[:, hidden:].astype(BF16)

    if between is not None:
        between()
    for window in range(windows):
        at = slice(window * cells, (window + 1) * cells)
        for pair in range(pairs):
            lanes = slice(pair * PAIR, (pair + 1) * PAIR)
            query = mixed_ref[at, lanes]
            keys = mixed_ref[at, hidden + pair * PAIR : hidden + (pair + 1) * PAIR]
            scores = dot(keys, spread(query), 1, 1) + bias_t_ref[:, lanes]
            scores_ref[at, lanes] = scores + closed[:, window : window + 1]
    for window in range(windows):
        at = slice(window * cells, (window + 1) * cells)
        scores = scores_ref[at, :]
        raised = jnp.exp(scores - jnp.max(scores, 0, keepdims=True))
        probs = raised * (1.0 / jnp.sum(raised, 0, keepdims=True))
        probs_low_ref[at, :] = probs.astype(BF16)
        if probs_ref is not None:
            probs_ref[at, :] = probs
    for window in range(windows):
        at = slice(window * cells, (window + 1) * cells)
        for pair in range(pairs):
            lanes = slice(pair * PAIR, (pair + 1) * PAIR)
            values = mixed_ref[at, 2 * hidden + pair * PAIR : 2 * hidden + (pair + 1) * PAIR]
            attended_ref[at, lanes] = own(dot(probs_low_ref[at, lanes], values, 0, 0)).astype(BF16)


def share_kernel(
    wet_hbm, bias_hbm, count_ref, x_hbm, g_hbm, qkv_hbm, held_ref, sent_ref,
    wet_ref, bias_ref, x_ref, g_ref, qkv_ref, mixed_ref, attended_ref, bias_t_ref, probs_low_ref, scores_ref,
    turned_ref, lines_ref, sems, *, sizes, outer, inner,
):
    rows, width = x_ref.shape
    cells = sizes[1]
    pairs = attended_ref.shape[1] // PAIR
    fetch = Fetch(sems)
    x_copy = fetch(x_hbm, x_ref)
    bias_copy = fetch(bias_hbm, bias_ref)
    wet_copy = fetch(wet_hbm, wet_ref)
    qkv_copy = fetch(qkv_hbm, qkv_ref)
    g_copy = fetch(g_hbm, g_ref)

    def small_waits():
        bias_copy.wait()
        wet_copy.wait()

    def turn():
        g_copy.wait()
        keep_live(g_ref, count_ref, cells)
        turned_ref[...] = g_ref[...].T

    attend(
        wet_ref, bias_ref, x_ref, qkv_ref, mixed_ref, attended_ref, None, probs_low_ref, scores_ref, bias_t_ref,
        None, None, x_copy.wait, small_waits, qkv_copy.wait, sizes, turn,
    )
    total = dot(turned_ref[...], attended_ref[...], 1, 0)
    half = width // 2
    for k in range(pairs):
        part = total[:, k * PAIR : (k + 1) * PAIR].reshape(outer, 2 * inner, PAIR)
        part = turned_by(part, FIRST_OUTER)
        part = jnp.transpose(part, (1, 0, 2)).reshape(inner, 2, outer, PAIR)
        part = turned_by(part, FIRST_INNER)
        for core in range(2):
            lines = pl.ds(core * half * pairs + k, half, stride=pairs)
            lines_ref[lines, :] = part[:, core].reshape(half, PAIR)
    core = lax.rem(lax.axis_index("dp"), 2)
    held = pl.ds(pl.multiple_of(core * half * pairs, half * pairs), half * pairs)
    sent = pl.ds(pl.multiple_of((1 - core) * half * pairs, half * pairs), half * pairs)
    held_ref[...] = lines_ref[held, :].astype(held_ref.dtype).reshape(held_ref.shape)
    sent_ref[...] = lines_ref[sent, :].astype(sent_ref.dtype).reshape(sent_ref.shape)


def grads_kernel(
    wet_hbm, bias_hbm, count_ref, x_hbm, g_hbm, qkv_hbm, proj_hbm, out_hbm, grad_hbm,
    wet_ref, bias_ref, x_ref, g_ref, qkv_ref, proj_ref, mixed_ref, attended_ref, bias_t_ref, probs_low_ref, scores_ref,
    probs_ref, normed_ref, inverse_ref, agrad_ref, mgrad_ref, out_ref, grad_ref,
    sems, *, sizes,
):
    windows, cells, heads = sizes
    rows, width = x_ref.shape
    hidden = proj_ref.shape[1]
    size = hidden // heads
    pairs = hidden // PAIR
    scale = size ** (-0.5)
    spread, own = make_spread(cells, size)
    fetch = Fetch(sems)
    x_copy = fetch(x_hbm, x_ref)
    bias_copy = fetch(bias_hbm, bias_ref)
    wet_copy = fetch(wet_hbm, wet_ref)
    qkv_copy = fetch(qkv_hbm, qkv_ref)
    g_copy = fetch(g_hbm, g_ref)
    proj_copy = fetch(proj_hbm, proj_ref)

    def small_waits():
        bias_copy.wait()
        wet_copy.wait()

    attend(
        wet_ref, bias_ref, x_ref, qkv_ref, mixed_ref, attended_ref, probs_ref, probs_low_ref, scores_ref, bias_t_ref,
        normed_ref, inverse_ref, x_copy.wait, small_waits, qkv_copy.wait, sizes,
    )
    g_copy.wait()
    keep_live(g_ref, count_ref, cells)
    proj_copy.wait()
    branch = dot(attended_ref[...], proj_ref[...], 1, 1)
    out_ref[...] = (x_ref[...].astype(F32) + branch).astype(BF16)
    keep_live(out_ref, count_ref, cells)
    out_copy = fetch(out_ref, out_hbm)
    agrad_ref[...] = dot(g_ref[...], proj_ref[...], 1, 0).astype(BF16)

    for window in range(windows):
        at = slice(window * cells, (window + 1) * cells)
        for pair in range(pairs):
            lanes = slice(pair * PAIR, (pair + 1) * PAIR)
            value_lanes = slice(2 * hidden + pair * PAIR, 2 * hidden + (pair + 1) * PAIR)
            agrad = spread(agrad_ref[at, lanes])
            scores_ref[at, lanes] = dot(mixed_ref[at, value_lanes], agrad, 1, 1)
            mgrad_ref[at, value_lanes] = dot(probs_low_ref[at, lanes], agrad, 1, 0).astype(BF16)
    for window in range(windows):
        at = slice(window * cells, (window + 1) * cells)
        probs = probs_ref[at, :]
        probs_grad = scores_ref[at, :]
        score_grad = probs * (probs_grad - jnp.sum(probs * probs_grad, 0, keepdims=True))
        probs_low_ref[at, :] = score_grad.astype(BF16)
    for window in range(windows):
        at = slice(window * cells, (window + 1) * cells)
        for pair in range(pairs):
            lanes = slice(pair * PAIR, (pair + 1) * PAIR)
            key_lanes = slice(hidden + pair * PAIR, hidden + (pair + 1) * PAIR)
            score_grad = probs_low_ref[at, lanes]
            query_grad = own(dot(score_grad, mixed_ref[at, key_lanes], 0, 0)) * scale
            mgrad_ref[at, lanes] = query_grad.astype(BF16)
            keys_grad = dot(score_grad, spread(mixed_ref[at, lanes]), 1, 0)
            mgrad_ref[at, key_lanes] = keys_grad.astype(BF16)

    normed_grad = dot(mgrad_ref[...], qkv_ref[...], 1, 1)
    normed = normed_ref[...]
    branch_grad = inverse_ref[...] * (
        normed_grad
        - jnp.mean(normed_grad, -1, keepdims=True)
        - normed * jnp.mean(normed_grad * normed, -1, keepdims=True)
    )
    grad_ref[...] = (g_ref[...].astype(F32) + branch_grad).astype(BF16)
    grad_copy = fetch(grad_ref, grad_hbm)
    out_copy.wait()
    grad_copy.wait()


def staging(x, g, wet, count, qkv_weight, score_bias):
    windows, cells, width = x.shape
    heads = score_bias.shape[0]
    hidden = qkv_weight.shape[1] // 3
    rows = windows * cells
    staged = [
        pltpu.VMEM((windows, cells), jnp.int32),
        pltpu.VMEM((heads * cells, cells), F32),
        pltpu.VMEM((rows, width), BF16),
        pltpu.VMEM((rows, width), BF16),
        pltpu.VMEM((width, 3 * hidden), BF16),
    ]
    worked = [
        pltpu.VMEM((rows, 3 * hidden), BF16),
        pltpu.VMEM((rows, hidden), BF16),
        pltpu.VMEM((cells, hidden), F32),
        pltpu.VMEM((rows, hidden), BF16),
        pltpu.VMEM((rows, hidden), F32),
    ]
    args = (
        wet,
        score_bias.reshape(heads * cells, cells),
        count,
        x.reshape(rows, width),
        g.reshape(rows, width),
        qkv_weight,
    )
    return args, staged, worked, (windows, cells, heads)


def placed(arrays):
    specs = [pl.BlockSpec(memory_space=pltpu.HBM)] * arrays
    return specs[:2] + [pl.BlockSpec(memory_space=pltpu.SMEM)] + specs[2:]


def pinned(args):
    return [
        arg if arg.size == 1 else pltpu.with_memory_space_constraint(arg, pltpu.HBM)
        for arg in args
    ]


def share_call(x, g, wet, count, qkv_weight, score_bias, outer, inner):
    args, staged, worked, sizes = staging(x, g, wet, count, qkv_weight, score_bias)
    rows, width = args[3].shape
    hidden = qkv_weight.shape[1] // 3
    pairs = hidden // PAIR
    return pl.pallas_call(
        functools.partial(share_kernel, sizes=sizes, outer=outer, inner=inner),
        out_shape=(
            pltpu.VMEM((inner, outer * pairs, PAIR), F32),
            pltpu.VMEM((inner, outer * pairs, PAIR), BF16),
        ),
        in_specs=placed(5),
        out_specs=[pl.BlockSpec(memory_space=pltpu.VMEM)] * 2,
        scratch_shapes=staged
        + worked
        + [
            pltpu.VMEM((width, rows), BF16),
            pltpu.VMEM((width * pairs + 8, PAIR), F32),
            pltpu.SemaphoreType.DMA((5,)),
        ],
        compiler_params=pltpu.CompilerParams(vmem_limit_bytes=VMEM_BYTES),
        cost_estimate=pl.CostEstimate(
            flops=2 * rows * width * 4 * hidden, bytes_accessed=4_000_000, transcendentals=200_000
        ),
    )(*pinned(args))


def grads_call(x, g, wet, count, qkv_weight, proj_weight, score_bias):
    args, staged, worked, sizes = staging(x, g, wet, count, qkv_weight, score_bias)
    rows, width = args[3].shape
    hidden = proj_weight.shape[1]
    hbm = pl.BlockSpec(memory_space=pltpu.HBM)
    flat = jax.ShapeDtypeStruct((rows, width), BF16)
    return pl.pallas_call(
        functools.partial(grads_kernel, sizes=sizes),
        out_shape=(flat, flat),
        in_specs=placed(6),
        out_specs=(hbm, hbm),
        scratch_shapes=staged
        + [pltpu.VMEM((width, hidden), BF16)]
        + worked
        + [
            pltpu.VMEM((rows, hidden), F32),
            pltpu.VMEM((rows, width), F32),
            pltpu.VMEM((rows, 1), F32),
            pltpu.VMEM((rows, hidden), BF16),
            pltpu.VMEM((rows, 3 * hidden), BF16),
            pltpu.VMEM((rows, width), BF16),
            pltpu.VMEM((rows, width), BF16),
            pltpu.SemaphoreType.DMA((8,)),
        ],
        compiler_params=pltpu.CompilerParams(vmem_limit_bytes=VMEM_BYTES),
        cost_estimate=pl.CostEstimate(
            flops=2 * rows * width * 16 * hidden, bytes_accessed=30_000_000, transcendentals=200_000
        ),
    )(*pinned(args + (proj_weight,)))


def shards(windows_in, cotangent, wet, count, qkv_weight, proj_weight, score_bias):
    outer, samples = lax.axis_size("space"), lax.axis_size("dp")
    inner = samples // 2
    pairs = proj_weight.shape[1] // PAIR
    x, g, wet = windows_in[0], cotangent[0], wet[0]
    held, sent = share_call(x, g, wet, count, qkv_weight, score_bias, outer, inner)
    got = lax.ppermute(sent, "dp", [(i, i ^ 1) for i in range(samples)])
    share = (held + got.astype(F32)).astype(BF16)
    wet, share = lax.optimization_barrier((wet, share))
    groups = [[2 * ((j + FIRST_INNER) % inner) + core for j in range(inner)] for core in range(2)]
    got = lax.all_to_all(share, "dp", 0, 0, tiled=True, axis_index_groups=groups)
    out, grad = grads_call(x, g, wet, count, qkv_weight, proj_weight, score_bias)
    got, out, grad = lax.optimization_barrier((got, out, grad))
    part = jnp.sum(got.astype(F32), 0).reshape(outer, pairs, PAIR)
    groups = [[(j + FIRST_OUTER) % outer for j in range(outer)]]
    got = lax.all_to_all(part, "space", 0, 0, tiled=True, axis_index_groups=groups)
    total = jnp.sum(got, 0).reshape(-1)
    return (out.reshape(windows_in.shape), grad.reshape(windows_in.shape), total)


def solution(mesh):
    in_specs = (
        P("dp", "space", None, None),
        P("dp", "space", None, None),
        P("dp", "space", None),
        P("dp", "space"),
        P(),
        P(),
        P(),
    )
    out_specs = (P("dp", "space", None, None), P("dp", "space", None, None), P(("space", "dp")))
    return jax.shard_map(shards, mesh=mesh, in_specs=in_specs, out_specs=out_specs, check_vma=False)
```

```python
import functools
import jax
import jax.numpy as jnp
from jax import lax
from jax.experimental import pallas as pl
from jax.experimental.pallas import tpu as pltpu
from jax.sharding import PartitionSpec as P

EPSILON = 1e-05
PAIR = 128
CORE_COLUMNS = ((1, 1), (0, 1), (1, 0), (0, 0))
COLUMNS = tuple((*column, core, odd) for core in (1, 0) for column in CORE_COLUMNS for odd in (1, 0))
FIRST_Z = 4
FIRST_Y = 4
VMEM_BYTES = 32 * 1024 * 1024
BF16 = jnp.bfloat16
F32 = jnp.float32


def dot(lhs, rhs, lhs_axis, rhs_axis):
    return lax.dot_general(
        lhs, rhs, (((lhs_axis,), (rhs_axis,)), ((), ())), preferred_element_type=F32
    )


def make_spread(cells, size):
    same_head = (
        lax.broadcasted_iota(jnp.int32, (PAIR, PAIR), 0) // size
        == lax.broadcasted_iota(jnp.int32, (PAIR, PAIR), 1) // size
    )
    first_head = lax.broadcasted_iota(jnp.int32, (cells, PAIR), 1) < size

    def spread(low):
        return jnp.where(same_head, jnp.concatenate([low, low], 0), jnp.zeros((), BF16))

    def own(both):
        return jnp.where(first_head, both[:cells], both[cells:])

    return spread, own


def turned_by(array, first, axis):
    before, after = jnp.split(array, [first], axis)
    return jnp.concatenate([after, before], axis)


def keep_live(ref, count_ref, cells):
    live = lax.broadcasted_iota(jnp.int32, (ref.shape[0], 1), 0) < count_ref[0, 0] * cells
    ref[...] = jnp.where(live, ref[...], jnp.zeros((), BF16))


class Fetch:
    def __init__(self, sems):
        self.sems = sems
        self.used = 0

    def __call__(self, source, target):
        copy = pltpu.make_async_copy(source, target, self.sems.at[self.used])
        self.used += 1
        copy.start()
        return copy


def attend(
    wet_ref, bias_ref, x_ref, qkv_ref, mixed_ref, attended_ref, probs_ref, probs_low_ref, scores_ref, bias_t_ref,
    normed_ref, inverse_ref, x_wait, small_waits, qkv_wait, sizes, between=None,
):
    windows, cells, heads = sizes
    hidden = attended_ref.shape[1]
    size = hidden // heads
    pairs = hidden // PAIR
    scale = size ** (-0.5)
    spread, own = make_spread(cells, size)

    x_wait()
    small_waits()
    bias_t_ref[...] = bias_ref[...].T
    closed = jnp.where(wet_ref[...] > 0, 0.0, -jnp.inf).astype(F32).T
    step = x_ref.shape[0] // 2
    lows = []
    for part in range(2):
        at = slice(part * step, (part + 1) * step)
        x_float = x_ref[at, :].astype(F32)
        centred = x_float - jnp.mean(x_float, -1, keepdims=True)
        inverse = lax.rsqrt(jnp.mean(centred * centred, -1, keepdims=True) + EPSILON)
        normed = centred * inverse
        if normed_ref is not None:
            normed_ref[at, :] = normed
            inverse_ref[at, :] = inverse
        lows.append(normed.astype(BF16))
    qkv_wait()
    for part in range(2):
        at = slice(part * step, (part + 1) * step)
        mixed = dot(lows[part], qkv_ref[...], 1, 0)
        mixed_ref[at, :hidden] = (mixed[:, :hidden] * scale).astype(BF16)
        mixed_ref[at, hidden:] = mixed[:, hidden:].astype(BF16)

    if between is not None:
        between()
    for window in range(windows):
        at = slice(window * cells, (window + 1) * cells)
        for pair in range(pairs):
            lanes = slice(pair * PAIR, (pair + 1) * PAIR)
            query = mixed_ref[at, lanes]
            keys = mixed_ref[at, hidden + pair * PAIR : hidden + (pair + 1) * PAIR]
            scores = dot(keys, spread(query), 1, 1) + bias_t_ref[:, lanes]
            scores_ref[at, lanes] = scores + closed[:, window : window + 1]
    for window in range(windows):
        at = slice(window * cells, (window + 1) * cells)
        scores = scores_ref[at, :]
        raised = jnp.exp(scores - jnp.max(scores, 0, keepdims=True))
        probs = raised * (1.0 / jnp.sum(raised, 0, keepdims=True))
        probs_low_ref[at, :] = probs.astype(BF16)
        if probs_ref is not None:
            probs_ref[at, :] = probs
    for window in range(windows):
        at = slice(window * cells, (window + 1) * cells)
        for pair in range(pairs):
            lanes = slice(pair * PAIR, (pair + 1) * PAIR)
            values = mixed_ref[at, 2 * hidden + pair * PAIR : 2 * hidden + (pair + 1) * PAIR]
            attended_ref[at, lanes] = own(dot(probs_low_ref[at, lanes], values, 0, 0)).astype(BF16)


def share_kernel(
    wet_hbm, bias_hbm, count_ref, x_hbm, g_hbm, qkv_hbm, share_hbm,
    wet_ref, bias_ref, x_ref, g_ref, qkv_ref, mixed_ref, attended_ref, bias_t_ref, probs_low_ref, scores_ref,
    turned_ref, total_ref, lines_ref, share_ref, sems, *, sizes, zs, ys,
):
    rows, width = x_ref.shape
    cells = sizes[1]
    pairs = attended_ref.shape[1] // PAIR
    fetch = Fetch(sems)
    x_copy = fetch(x_hbm, x_ref)
    bias_copy = fetch(bias_hbm, bias_ref)
    wet_copy = fetch(wet_hbm, wet_ref)
    qkv_copy = fetch(qkv_hbm, qkv_ref)
    g_copy = fetch(g_hbm, g_ref)

    def small_waits():
        bias_copy.wait()
        wet_copy.wait()

    def turn():
        g_copy.wait()
        keep_live(g_ref, count_ref, cells)
        turned_ref[...] = g_ref[...].T

    attend(
        wet_ref, bias_ref, x_ref, qkv_ref, mixed_ref, attended_ref, None, probs_low_ref, scores_ref, bias_t_ref,
        None, None, x_copy.wait, small_waits, qkv_copy.wait, sizes, turn,
    )
    total = dot(turned_ref[...], attended_ref[...], 1, 0)
    for k in range(pairs):
        total_ref[k, :width, :] = total[:, k * PAIR : (k + 1) * PAIR]
    lines = zs // 2 * ys * pairs
    copies = []
    for core in (1, 0):
        for k in range(pairs):
            part = total_ref[k, pl.ds(core, width // 2, stride=2), :].reshape(zs * 4, ys, PAIR)
            part = turned_by(part, FIRST_Y, 1).reshape(zs // 2, 8, ys, PAIR)
            part = turned_by(part, FIRST_Z, 0)
            for column in range(8):
                odd, xlo, xhi = column // 4, column // 2 % 2, column % 2
                first = COLUMNS.index((xlo, xhi, core, odd)) * lines + k
                lines_ref[pl.ds(first, lines // pairs, stride=pairs), :] = part[:, column].reshape(lines // pairs, PAIR)
        first = 8 * (1 - core)
        done = lines_ref[first * lines : (first + 8) * lines, :].astype(BF16)
        share_ref[first : first + 8] = done.reshape(8, lines, PAIR)
        at = slice(first, first + 8)
        copies.append(fetch(share_ref.at[at], share_hbm.at[at]))
    for copy in copies:
        copy.wait()


def grads_kernel(
    wet_hbm, bias_hbm, count_ref, x_hbm, g_hbm, qkv_hbm, proj_hbm, out_hbm, grad_hbm,
    wet_ref, bias_ref, x_ref, g_ref, qkv_ref, proj_ref, mixed_ref, attended_ref, bias_t_ref, probs_low_ref, scores_ref,
    probs_ref, normed_ref, inverse_ref, agrad_ref, mgrad_ref, out_ref, grad_ref,
    sems, *, sizes,
):
    windows, cells, heads = sizes
    rows, width = x_ref.shape
    hidden = proj_ref.shape[1]
    size = hidden // heads
    pairs = hidden // PAIR
    scale = size ** (-0.5)
    spread, own = make_spread(cells, size)
    fetch = Fetch(sems)
    x_copy = fetch(x_hbm, x_ref)
    bias_copy = fetch(bias_hbm, bias_ref)
    wet_copy = fetch(wet_hbm, wet_ref)
    qkv_copy = fetch(qkv_hbm, qkv_ref)
    g_copy = fetch(g_hbm, g_ref)
    proj_copy = fetch(proj_hbm, proj_ref)

    def small_waits():
        bias_copy.wait()
        wet_copy.wait()

    attend(
        wet_ref, bias_ref, x_ref, qkv_ref, mixed_ref, attended_ref, probs_ref, probs_low_ref, scores_ref, bias_t_ref,
        normed_ref, inverse_ref, x_copy.wait, small_waits, qkv_copy.wait, sizes,
    )
    g_copy.wait()
    keep_live(g_ref, count_ref, cells)
    proj_copy.wait()
    branch = dot(attended_ref[...], proj_ref[...], 1, 1)
    out_ref[...] = (x_ref[...].astype(F32) + branch).astype(BF16)
    keep_live(out_ref, count_ref, cells)
    out_copy = fetch(out_ref, out_hbm)
    agrad_ref[...] = dot(g_ref[...], proj_ref[...], 1, 0).astype(BF16)

    for window in range(windows):
        at = slice(window * cells, (window + 1) * cells)
        for pair in range(pairs):
            lanes = slice(pair * PAIR, (pair + 1) * PAIR)
            value_lanes = slice(2 * hidden + pair * PAIR, 2 * hidden + (pair + 1) * PAIR)
            agrad = spread(agrad_ref[at, lanes])
            scores_ref[at, lanes] = dot(mixed_ref[at, value_lanes], agrad, 1, 1)
            mgrad_ref[at, value_lanes] = dot(probs_low_ref[at, lanes], agrad, 1, 0).astype(BF16)
    for window in range(windows):
        at = slice(window * cells, (window + 1) * cells)
        probs = probs_ref[at, :]
        probs_grad = scores_ref[at, :]
        score_grad = probs * (probs_grad - jnp.sum(probs * probs_grad, 0, keepdims=True))
        probs_low_ref[at, :] = score_grad.astype(BF16)
    for window in range(windows):
        at = slice(window * cells, (window + 1) * cells)
        for pair in range(pairs):
            lanes = slice(pair * PAIR, (pair + 1) * PAIR)
            key_lanes = slice(hidden + pair * PAIR, hidden + (pair + 1) * PAIR)
            score_grad = probs_low_ref[at, lanes]
            query_grad = own(dot(score_grad, mixed_ref[at, key_lanes], 0, 0)) * scale
            mgrad_ref[at, lanes] = query_grad.astype(BF16)
            keys_grad = dot(score_grad, spread(mixed_ref[at, lanes]), 1, 0)
            mgrad_ref[at, key_lanes] = keys_grad.astype(BF16)

    normed_grad = dot(mgrad_ref[...], qkv_ref[...], 1, 1)
    normed = normed_ref[...]
    branch_grad = inverse_ref[...] * (
        normed_grad
        - jnp.mean(normed_grad, -1, keepdims=True)
        - normed * jnp.mean(normed_grad * normed, -1, keepdims=True)
    )
    grad_ref[...] = (g_ref[...].astype(F32) + branch_grad).astype(BF16)
    grad_copy = fetch(grad_ref, grad_hbm)
    out_copy.wait()
    grad_copy.wait()


def staging(x, g, wet, count, qkv_weight, score_bias):
    windows, cells, width = x.shape
    heads = score_bias.shape[0]
    hidden = qkv_weight.shape[1] // 3
    rows = windows * cells
    staged = [
        pltpu.VMEM((windows, cells), jnp.int32),
        pltpu.VMEM((heads * cells, cells), F32),
        pltpu.VMEM((rows, width), BF16),
        pltpu.VMEM((rows, width), BF16),
        pltpu.VMEM((width, 3 * hidden), BF16),
    ]
    worked = [
        pltpu.VMEM((rows, 3 * hidden), BF16),
        pltpu.VMEM((rows, hidden), BF16),
        pltpu.VMEM((cells, hidden), F32),
        pltpu.VMEM((rows, hidden), BF16),
        pltpu.VMEM((rows, hidden), F32),
    ]
    args = (
        wet,
        score_bias.reshape(heads * cells, cells),
        count,
        x.reshape(rows, width),
        g.reshape(rows, width),
        qkv_weight,
    )
    return args, staged, worked, (windows, cells, heads)


def placed(arrays):
    specs = [pl.BlockSpec(memory_space=pltpu.HBM)] * arrays
    return specs[:2] + [pl.BlockSpec(memory_space=pltpu.SMEM)] + specs[2:]


def pinned(args):
    return [
        arg if arg.size == 1 else pltpu.with_memory_space_constraint(arg, pltpu.HBM)
        for arg in args
    ]


def share_call(x, g, wet, count, qkv_weight, score_bias, zs, ys):
    args, staged, worked, sizes = staging(x, g, wet, count, qkv_weight, score_bias)
    rows, width = args[3].shape
    hidden = qkv_weight.shape[1] // 3
    pairs = hidden // PAIR
    return pl.pallas_call(
        functools.partial(share_kernel, sizes=sizes, zs=zs, ys=ys),
        out_shape=pltpu.HBM((16, zs // 2 * ys * pairs, PAIR), BF16),
        in_specs=placed(5),
        out_specs=pl.BlockSpec(memory_space=pltpu.HBM),
        scratch_shapes=staged
        + worked
        + [
            pltpu.VMEM((width, rows), BF16),
            pltpu.VMEM((pairs, width + 8, PAIR), F32),
            pltpu.VMEM((width * pairs + 8, PAIR), F32),
            pltpu.VMEM((16, zs // 2 * ys * pairs, PAIR), BF16),
            pltpu.SemaphoreType.DMA((7,)),
        ],
        compiler_params=pltpu.CompilerParams(vmem_limit_bytes=VMEM_BYTES),
        cost_estimate=pl.CostEstimate(
            flops=2 * rows * width * 4 * hidden, bytes_accessed=4_000_000, transcendentals=200_000
        ),
    )(*pinned(args))


def grads_call(x, g, wet, count, qkv_weight, proj_weight, score_bias):
    args, staged, worked, sizes = staging(x, g, wet, count, qkv_weight, score_bias)
    rows, width = args[3].shape
    hidden = proj_weight.shape[1]
    hbm = pl.BlockSpec(memory_space=pltpu.HBM)
    flat = jax.ShapeDtypeStruct((rows, width), BF16)
    return pl.pallas_call(
        functools.partial(grads_kernel, sizes=sizes),
        out_shape=(flat, flat),
        in_specs=placed(6),
        out_specs=(hbm, hbm),
        scratch_shapes=staged
        + [pltpu.VMEM((width, hidden), BF16)]
        + worked
        + [
            pltpu.VMEM((rows, hidden), F32),
            pltpu.VMEM((rows, width), F32),
            pltpu.VMEM((rows, 1), F32),
            pltpu.VMEM((rows, hidden), BF16),
            pltpu.VMEM((rows, 3 * hidden), BF16),
            pltpu.VMEM((rows, width), BF16),
            pltpu.VMEM((rows, width), BF16),
            pltpu.SemaphoreType.DMA((8,)),
        ],
        compiler_params=pltpu.CompilerParams(vmem_limit_bytes=VMEM_BYTES),
        cost_estimate=pl.CostEstimate(
            flops=2 * rows * width * 16 * hidden, bytes_accessed=30_000_000, transcendentals=200_000
        ),
    )(*pinned(args + (proj_weight,)))


def shards(windows_in, cotangent, wet, count, qkv_weight, proj_weight, score_bias):
    zs, ys = lax.axis_size("space") // 2, lax.axis_size("dp") // 4
    both = ("space", "dp")
    pairs = proj_weight.shape[1] // PAIR
    x, g, wet = windows_in[0], cotangent[0], wet[0]

    def device(half_z, y, column):
        xlo, xhi, core, odd = column
        return ((((2 * half_z + odd) * 2 + xlo) * 2 + xhi) * ys + y) * 2 + core

    half = zs // 2
    places = [((FIRST_Z + i) % half, (FIRST_Y + j) % ys) for i in range(half) for j in range(ys)]
    near = [[device(*place, column) for column in COLUMNS] for place in places]
    far = [[device(*place, column) for place in places] for column in COLUMNS]
    share = share_call(x, g, wet, count, qkv_weight, score_bias, zs, ys)
    wet, share = lax.optimization_barrier((wet, share))
    got = lax.all_to_all(share, both, 0, 0, tiled=True, axis_index_groups=near)
    out, grad = grads_call(x, g, wet, count, qkv_weight, proj_weight, score_bias)
    got, out, grad = lax.optimization_barrier((got, out, grad))
    part = jnp.sum(got.astype(F32), 0).astype(BF16).reshape(half * ys, pairs, PAIR)
    got = lax.all_to_all(part, both, 0, 0, tiled=True, axis_index_groups=far)
    total = jnp.sum(got.astype(F32), 0).reshape(-1)
    return (out.reshape(windows_in.shape), grad.reshape(windows_in.shape), total)


def solution(mesh):
    in_specs = (
        P("dp", "space", None, None),
        P("dp", "space", None, None),
        P("dp", "space", None),
        P("dp", "space"),
        P(),
        P(),
        P(),
    )
    out_specs = (P("dp", "space", None, None), P("dp", "space", None, None), P(("space", "dp")))
    return jax.shard_map(shards, mesh=mesh, in_specs=in_specs, out_specs=out_specs, check_vma=False)
```

```python
import functools
import jax
import jax.numpy as jnp
from jax import lax
from jax.experimental import pallas as pl
from jax.experimental.pallas import tpu as pltpu
from jax.sharding import PartitionSpec as P

EPSILON = 1e-05
PAIR = 128
CORE_COLUMNS = ((1, 1), (0, 1), (1, 0), (0, 0))
COLUMNS = tuple((*column, core, odd) for core in (1, 0) for column in CORE_COLUMNS for odd in (1, 0))
FIRST_Z = 4
FIRST_Y = 4
VMEM_BYTES = 32 * 1024 * 1024
BF16 = jnp.bfloat16
F32 = jnp.float32


def dot(lhs, rhs, lhs_axis, rhs_axis):
    return lax.dot_general(
        lhs, rhs, (((lhs_axis,), (rhs_axis,)), ((), ())), preferred_element_type=F32
    )


def make_spread(cells, size):
    same_head = (
        lax.broadcasted_iota(jnp.int32, (PAIR, PAIR), 0) // size
        == lax.broadcasted_iota(jnp.int32, (PAIR, PAIR), 1) // size
    )
    first_head = lax.broadcasted_iota(jnp.int32, (cells, PAIR), 1) < size

    def spread(low):
        return jnp.where(same_head, jnp.concatenate([low, low], 0), jnp.zeros((), BF16))

    def own(both):
        return jnp.where(first_head, both[:cells], both[cells:])

    return spread, own


def turned_by(array, first, axis):
    before, after = jnp.split(array, [first], axis)
    return jnp.concatenate([after, before], axis)


def downward(count):
    return [(FIRST_Z - i) % count for i in range(count)]


def keep_live(ref, count_ref, cells):
    live = lax.broadcasted_iota(jnp.int32, (ref.shape[0], 1), 0) < count_ref[0, 0] * cells
    ref[...] = jnp.where(live, ref[...], jnp.zeros((), BF16))


class Fetch:
    def __init__(self, sems):
        self.sems = sems
        self.used = 0

    def __call__(self, source, target):
        copy = pltpu.make_async_copy(source, target, self.sems.at[self.used])
        self.used += 1
        copy.start()
        return copy


def attend(
    wet_ref, bias_ref, x_ref, qkv_ref, mixed_ref, attended_ref, probs_ref, probs_low_ref, scores_ref, bias_t_ref,
    normed_ref, inverse_ref, x_wait, small_waits, qkv_wait, sizes, between=None,
):
    windows, cells, heads = sizes
    hidden = attended_ref.shape[1]
    size = hidden // heads
    pairs = hidden // PAIR
    scale = size ** (-0.5)
    spread, own = make_spread(cells, size)

    x_wait()
    small_waits()
    bias_t_ref[...] = bias_ref[...].T
    closed = jnp.where(wet_ref[...] > 0, 0.0, -jnp.inf).astype(F32).T
    step = x_ref.shape[0] // 2
    lows = []
    for part in range(2):
        at = slice(part * step, (part + 1) * step)
        x_float = x_ref[at, :].astype(F32)
        centred = x_float - jnp.mean(x_float, -1, keepdims=True)
        inverse = lax.rsqrt(jnp.mean(centred * centred, -1, keepdims=True) + EPSILON)
        normed = centred * inverse
        if normed_ref is not None:
            normed_ref[at, :] = normed
            inverse_ref[at, :] = inverse
        lows.append(normed.astype(BF16))
    qkv_wait()
    for part in range(2):
        at = slice(part * step, (part + 1) * step)
        mixed = dot(lows[part], qkv_ref[...], 1, 0)
        mixed_ref[at, :hidden] = (mixed[:, :hidden] * scale).astype(BF16)
        mixed_ref[at, hidden:] = mixed[:, hidden:].astype(BF16)

    if between is not None:
        between()
    for window in range(windows):
        at = slice(window * cells, (window + 1) * cells)
        for pair in range(pairs):
            lanes = slice(pair * PAIR, (pair + 1) * PAIR)
            query = mixed_ref[at, lanes]
            keys = mixed_ref[at, hidden + pair * PAIR : hidden + (pair + 1) * PAIR]
            scores = dot(keys, spread(query), 1, 1) + bias_t_ref[:, lanes]
            scores_ref[at, lanes] = scores + closed[:, window : window + 1]
    for window in range(windows):
        at = slice(window * cells, (window + 1) * cells)
        scores = scores_ref[at, :]
        raised = jnp.exp(scores - jnp.max(scores, 0, keepdims=True))
        probs = raised * (1.0 / jnp.sum(raised, 0, keepdims=True))
        probs_low_ref[at, :] = probs.astype(BF16)
        if probs_ref is not None:
            probs_ref[at, :] = probs
    for window in range(windows):
        at = slice(window * cells, (window + 1) * cells)
        for pair in range(pairs):
            lanes = slice(pair * PAIR, (pair + 1) * PAIR)
            values = mixed_ref[at, 2 * hidden + pair * PAIR : 2 * hidden + (pair + 1) * PAIR]
            attended_ref[at, lanes] = own(dot(probs_low_ref[at, lanes], values, 0, 0)).astype(BF16)


def share_kernel(
    wet_hbm, bias_hbm, count_ref, x_hbm, g_hbm, qkv_hbm, share_hbm,
    wet_ref, bias_ref, x_ref, g_ref, qkv_ref, mixed_ref, attended_ref, bias_t_ref, probs_low_ref, scores_ref,
    turned_ref, total_ref, lines_ref, share_ref, sems, *, sizes, zs, ys,
):
    rows, width = x_ref.shape
    cells = sizes[1]
    pairs = attended_ref.shape[1] // PAIR
    fetch = Fetch(sems)
    x_copy = fetch(x_hbm, x_ref)
    bias_copy = fetch(bias_hbm, bias_ref)
    wet_copy = fetch(wet_hbm, wet_ref)
    qkv_copy = fetch(qkv_hbm, qkv_ref)
    g_copy = fetch(g_hbm, g_ref)

    def small_waits():
        bias_copy.wait()
        wet_copy.wait()

    def turn():
        g_copy.wait()
        keep_live(g_ref, count_ref, cells)
        turned_ref[...] = g_ref[...].T

    attend(
        wet_ref, bias_ref, x_ref, qkv_ref, mixed_ref, attended_ref, None, probs_low_ref, scores_ref, bias_t_ref,
        None, None, x_copy.wait, small_waits, qkv_copy.wait, sizes, turn,
    )
    total = dot(turned_ref[...], attended_ref[...], 1, 0)
    for k in range(pairs):
        total_ref[k, :width, :] = total[:, k * PAIR : (k + 1) * PAIR]
    lines = zs // 2 * ys * pairs
    copies = []
    for core in (1, 0):
        for k in range(pairs):
            part = total_ref[k, pl.ds(core, width // 2, stride=2), :].reshape(zs * 4, ys, PAIR)
            part = turned_by(part, FIRST_Y, 1).reshape(zs // 2, 8, ys, PAIR)
            part = jnp.concatenate([part[z : z + 1] for z in downward(zs // 2)], 0)
            for column in range(8):
                odd, xlo, xhi = column // 4, column // 2 % 2, column % 2
                first = COLUMNS.index((xlo, xhi, core, odd)) * lines + k
                lines_ref[pl.ds(first, lines // pairs, stride=pairs), :] = part[:, column].reshape(lines // pairs, PAIR)
        first = 8 * (1 - core)
        done = lines_ref[first * lines : (first + 8) * lines, :].astype(BF16)
        share_ref[first : first + 8] = done.reshape(8, lines, PAIR)
        at = slice(first, first + 8)
        copies.append(fetch(share_ref.at[at], share_hbm.at[at]))
    for copy in copies:
        copy.wait()


def grads_kernel(
    wet_hbm, bias_hbm, count_ref, x_hbm, g_hbm, qkv_hbm, proj_hbm, out_hbm, grad_hbm,
    wet_ref, bias_ref, x_ref, g_ref, qkv_ref, proj_ref, mixed_ref, attended_ref, bias_t_ref, probs_low_ref, scores_ref,
    probs_ref, normed_ref, inverse_ref, agrad_ref, mgrad_ref, out_ref, grad_ref,
    sems, *, sizes,
):
    windows, cells, heads = sizes
    rows, width = x_ref.shape
    hidden = proj_ref.shape[1]
    size = hidden // heads
    pairs = hidden // PAIR
    scale = size ** (-0.5)
    spread, own = make_spread(cells, size)
    fetch = Fetch(sems)
    x_copy = fetch(x_hbm, x_ref)
    bias_copy = fetch(bias_hbm, bias_ref)
    wet_copy = fetch(wet_hbm, wet_ref)
    qkv_copy = fetch(qkv_hbm, qkv_ref)
    g_copy = fetch(g_hbm, g_ref)
    proj_copy = fetch(proj_hbm, proj_ref)

    def small_waits():
        bias_copy.wait()
        wet_copy.wait()

    attend(
        wet_ref, bias_ref, x_ref, qkv_ref, mixed_ref, attended_ref, probs_ref, probs_low_ref, scores_ref, bias_t_ref,
        normed_ref, inverse_ref, x_copy.wait, small_waits, qkv_copy.wait, sizes,
    )
    g_copy.wait()
    keep_live(g_ref, count_ref, cells)
    proj_copy.wait()
    branch = dot(attended_ref[...], proj_ref[...], 1, 1)
    out_ref[...] = (x_ref[...].astype(F32) + branch).astype(BF16)
    keep_live(out_ref, count_ref, cells)
    out_copy = fetch(out_ref, out_hbm)
    agrad_ref[...] = dot(g_ref[...], proj_ref[...], 1, 0).astype(BF16)

    for window in range(windows):
        at = slice(window * cells, (window + 1) * cells)
        for pair in range(pairs):
            lanes = slice(pair * PAIR, (pair + 1) * PAIR)
            value_lanes = slice(2 * hidden + pair * PAIR, 2 * hidden + (pair + 1) * PAIR)
            agrad = spread(agrad_ref[at, lanes])
            scores_ref[at, lanes] = dot(mixed_ref[at, value_lanes], agrad, 1, 1)
            mgrad_ref[at, value_lanes] = dot(probs_low_ref[at, lanes], agrad, 1, 0).astype(BF16)
    for window in range(windows):
        at = slice(window * cells, (window + 1) * cells)
        probs = probs_ref[at, :]
        probs_grad = scores_ref[at, :]
        score_grad = probs * (probs_grad - jnp.sum(probs * probs_grad, 0, keepdims=True))
        probs_low_ref[at, :] = score_grad.astype(BF16)
    for window in range(windows):
        at = slice(window * cells, (window + 1) * cells)
        for pair in range(pairs):
            lanes = slice(pair * PAIR, (pair + 1) * PAIR)
            key_lanes = slice(hidden + pair * PAIR, hidden + (pair + 1) * PAIR)
            score_grad = probs_low_ref[at, lanes]
            query_grad = own(dot(score_grad, mixed_ref[at, key_lanes], 0, 0)) * scale
            mgrad_ref[at, lanes] = query_grad.astype(BF16)
            keys_grad = dot(score_grad, spread(mixed_ref[at, lanes]), 1, 0)
            mgrad_ref[at, key_lanes] = keys_grad.astype(BF16)

    normed_grad = dot(mgrad_ref[...], qkv_ref[...], 1, 1)
    normed = normed_ref[...]
    branch_grad = inverse_ref[...] * (
        normed_grad
        - jnp.mean(normed_grad, -1, keepdims=True)
        - normed * jnp.mean(normed_grad * normed, -1, keepdims=True)
    )
    grad_ref[...] = (g_ref[...].astype(F32) + branch_grad).astype(BF16)
    grad_copy = fetch(grad_ref, grad_hbm)
    out_copy.wait()
    grad_copy.wait()


def staging(x, g, wet, count, qkv_weight, score_bias):
    windows, cells, width = x.shape
    heads = score_bias.shape[0]
    hidden = qkv_weight.shape[1] // 3
    rows = windows * cells
    staged = [
        pltpu.VMEM((windows, cells), jnp.int32),
        pltpu.VMEM((heads * cells, cells), F32),
        pltpu.VMEM((rows, width), BF16),
        pltpu.VMEM((rows, width), BF16),
        pltpu.VMEM((width, 3 * hidden), BF16),
    ]
    worked = [
        pltpu.VMEM((rows, 3 * hidden), BF16),
        pltpu.VMEM((rows, hidden), BF16),
        pltpu.VMEM((cells, hidden), F32),
        pltpu.VMEM((rows, hidden), BF16),
        pltpu.VMEM((rows, hidden), F32),
    ]
    args = (
        wet,
        score_bias.reshape(heads * cells, cells),
        count,
        x.reshape(rows, width),
        g.reshape(rows, width),
        qkv_weight,
    )
    return args, staged, worked, (windows, cells, heads)


def placed(arrays):
    specs = [pl.BlockSpec(memory_space=pltpu.HBM)] * arrays
    return specs[:2] + [pl.BlockSpec(memory_space=pltpu.SMEM)] + specs[2:]


def pinned(args):
    return [
        arg if arg.size == 1 else pltpu.with_memory_space_constraint(arg, pltpu.HBM)
        for arg in args
    ]


def share_call(x, g, wet, count, qkv_weight, score_bias, zs, ys):
    args, staged, worked, sizes = staging(x, g, wet, count, qkv_weight, score_bias)
    rows, width = args[3].shape
    hidden = qkv_weight.shape[1] // 3
    pairs = hidden // PAIR
    return pl.pallas_call(
        functools.partial(share_kernel, sizes=sizes, zs=zs, ys=ys),
        out_shape=pltpu.HBM((16, zs // 2 * ys * pairs, PAIR), BF16),
        in_specs=placed(5),
        out_specs=pl.BlockSpec(memory_space=pltpu.HBM),
        scratch_shapes=staged
        + worked
        + [
            pltpu.VMEM((width, rows), BF16),
            pltpu.VMEM((pairs, width + 8, PAIR), F32),
            pltpu.VMEM((width * pairs + 8, PAIR), F32),
            pltpu.VMEM((16, zs // 2 * ys * pairs, PAIR), BF16),
            pltpu.SemaphoreType.DMA((7,)),
        ],
        compiler_params=pltpu.CompilerParams(vmem_limit_bytes=VMEM_BYTES),
        cost_estimate=pl.CostEstimate(
            flops=2 * rows * width * 4 * hidden, bytes_accessed=4_000_000, transcendentals=200_000
        ),
    )(*pinned(args))


def grads_call(x, g, wet, count, qkv_weight, proj_weight, score_bias):
    args, staged, worked, sizes = staging(x, g, wet, count, qkv_weight, score_bias)
    rows, width = args[3].shape
    hidden = proj_weight.shape[1]
    hbm = pl.BlockSpec(memory_space=pltpu.HBM)
    flat = jax.ShapeDtypeStruct((rows, width), BF16)
    return pl.pallas_call(
        functools.partial(grads_kernel, sizes=sizes),
        out_shape=(flat, flat),
        in_specs=placed(6),
        out_specs=(hbm, hbm),
        scratch_shapes=staged
        + [pltpu.VMEM((width, hidden), BF16)]
        + worked
        + [
            pltpu.VMEM((rows, hidden), F32),
            pltpu.VMEM((rows, width), F32),
            pltpu.VMEM((rows, 1), F32),
            pltpu.VMEM((rows, hidden), BF16),
            pltpu.VMEM((rows, 3 * hidden), BF16),
            pltpu.VMEM((rows, width), BF16),
            pltpu.VMEM((rows, width), BF16),
            pltpu.SemaphoreType.DMA((8,)),
        ],
        compiler_params=pltpu.CompilerParams(vmem_limit_bytes=VMEM_BYTES),
        cost_estimate=pl.CostEstimate(
            flops=2 * rows * width * 16 * hidden, bytes_accessed=30_000_000, transcendentals=200_000
        ),
    )(*pinned(args + (proj_weight,)))


def shards(windows_in, cotangent, wet, count, qkv_weight, proj_weight, score_bias):
    zs, ys = lax.axis_size("space") // 2, lax.axis_size("dp") // 4
    both = ("space", "dp")
    pairs = proj_weight.shape[1] // PAIR
    x, g, wet = windows_in[0], cotangent[0], wet[0]

    def device(half_z, y, column):
        xlo, xhi, core, odd = column
        return ((((2 * half_z + odd) * 2 + xlo) * 2 + xhi) * ys + y) * 2 + core

    half = zs // 2
    places = [(z, (FIRST_Y + j) % ys) for z in downward(half) for j in range(ys)]
    near = [[device(*place, column) for column in COLUMNS] for place in places]
    far = [[device(*place, column) for place in places] for column in COLUMNS]
    share = share_call(x, g, wet, count, qkv_weight, score_bias, zs, ys)
    wet, share = lax.optimization_barrier((wet, share))
    got = lax.all_to_all(share, both, 0, 0, tiled=True, axis_index_groups=near)
    out, grad = grads_call(x, g, wet, count, qkv_weight, proj_weight, score_bias)
    got, out, grad = lax.optimization_barrier((got, out, grad))
    part = jnp.sum(got.astype(F32), 0).astype(BF16).reshape(half * ys, pairs, PAIR)
    got = lax.all_to_all(part, both, 0, 0, tiled=True, axis_index_groups=far)
    total = jnp.sum(got.astype(F32), 0).reshape(-1)
    return (out.reshape(windows_in.shape), grad.reshape(windows_in.shape), total)


def solution(mesh):
    in_specs = (
        P("dp", "space", None, None),
        P("dp", "space", None, None),
        P("dp", "space", None),
        P("dp", "space"),
        P(),
        P(),
        P(),
    )
    out_specs = (P("dp", "space", None, None), P("dp", "space", None, None), P(("space", "dp")))
    return jax.shard_map(shards, mesh=mesh, in_specs=in_specs, out_specs=out_specs, check_vma=False)
```
